32 devices in a mesh: groups: 2 (over x), col: 16 (over z, y, core).
Axes of the slice: x: 2, y: 2, z: 4, core: 2. Of those that a mesh axis runs over, the one named last changes fastest.
Arguments:
- coords: bfloat16 [3, 131072], P(None, ('groups', 'col')), parts along dimension 1, may hold values from 0 to 8
- probes: bfloat16 [64, 131072], P(None, ('groups', 'col')), parts along dimension 1, may hold values from -6 to 6
- order: int32 [131072], P(('groups', 'col')), parts along dimension 0, may hold values from 0 to 65535, as said below
- near_list: int32 [512, 27], P(('groups', 'col')), parts along dimension 0, may hold values from -16 to 271, as said below
- near_count: int32 [512], P(('groups', 'col')), parts along dimension 0, may hold values from 1 to 27
- leaf_basis: bfloat16 [512, 64, 256], P(('groups', 'col')), parts along dimension 0, may hold values from -0.375 to 0.375
- transfer_low: bfloat16 [512, 64, 64], P(('groups', 'col')), parts along dimension 0, may hold values from -0.5 to 0.5
- transfer_top: bfloat16 [256, 64, 64], P(('groups', 'col')), parts along dimension 0, may hold values from -0.5 to 0.5
- coupling_leaf: bfloat16 [512, 16, 64, 64], P(('groups', 'col')), parts along dimension 0, may hold values from -0.1875 to 0.1875
- coupling_mid: bfloat16 [256, 16, 64, 64], P(('groups', 'col')), parts along dimension 0, may hold values from -0.1875 to 0.1875
- coupling_top: bfloat16 [128, 16, 64, 64], P(('groups', 'col')), parts along dimension 0, may hold values from -0.1875 to 0.1875
- far_leaf: int32 [512, 16], P(('groups', 'col')), parts along dimension 0, may hold values from -16 to 271, as said below
- far_mid: int32 [256, 16], P(('groups', 'col')), parts along dimension 0, may hold values from -8 to 135, as said below
- far_top: int32 [128, 16], P(('groups', 'col')), parts along dimension 0, may hold values from 0 to 63, as said below
Outputs:
- kernel_product: float32 [64, 131072], P(None, ('groups', 'col')), parts along dimension 1
The draws below stay inside these ranges and needn't reach their ends.
There are 2 independent parts, one for each index of `groups`. The reference program is written for one: setup_inputs(seed, part) draws one part's arguments, and reference() takes and returns one part's arrays. A program takes and returns all parts, laid end to end along the dimension named above; each array names one. Nothing has to cross between parts.
Inputs may be any that keep to these rules, and one draw needn't show every extreme that they name: `order`: each aligned block of 4096 entries is a permutation of that block's own positions. `near_list`: slot 0 of leaf i names i itself; every entry lies within 16 of its leaf's index. `far_leaf`: every entry lies within 16 of its cluster's index. `far_mid`: every entry lies within 8 of its cluster's index. `far_top`: in each aligned block of 4 rows, the entries name at most one cluster of each aligned range of 4 top-level clusters.
All inputs are finite; a program needn't handle non-finite values.
Results may differ from the reference program's by a relative error of at most 0.0034.
The reference program's roundings to bfloat16 on the way count: a program that leaves them out, or rounds other values in their place, can miss the bound.
Values may be sent and summed in bfloat16 or wider, within the bound.
A program may use at most 128 MiB of HBM per device.

```python
import math
import jax
import jax.numpy as jnp
from jax import lax

LEAF = 256
PROBES = 64
RANK = 64
LEAF_DEV = 16
NEAR = 27
FAR = 16
LEAVES = 256
NPTS = 65536
PTS_DEV = 4096


def draw_order(key, part):
    key = jax.random.fold_in(key, 11)
    block_total = NPTS // PTS_DEV
    block_keys = jax.random.split(key, block_total)
    shuffled = jax.vmap(lambda single: jax.random.permutation(single, PTS_DEV))(block_keys)
    offsets = (jnp.arange(block_total, dtype=jnp.int32) * PTS_DEV)[:, None]
    return (shuffled.astype(jnp.int32) + offsets).reshape(NPTS)


def draw_near_list(key, part):
    key = jax.random.fold_in(key, 23)
    shifts = jax.random.randint(key, (LEAVES, NEAR), -LEAF_DEV, LEAF_DEV + 1, dtype=jnp.int32)
    shifts = shifts.at[:, 0].set(0)
    return jnp.arange(LEAVES, dtype=jnp.int32)[:, None] + shifts


def draw_near_count(key, part):
    key = jax.random.fold_in(key, 37)
    first_key, second_key = jax.random.split(key)
    counts = jax.random.randint(first_key, (LEAVES,), 1, NEAR + 1, dtype=jnp.int32)
    chosen = jax.random.randint(second_key, (), 0, LEAVES, dtype=jnp.int32)
    return jnp.where(jnp.arange(LEAVES, dtype=jnp.int32) == chosen, NEAR, counts)


def draw_far_leaf(key, part):
    key = jax.random.fold_in(key, 41)
    shifts = jax.random.randint(key, (LEAVES, FAR), -LEAF_DEV, LEAF_DEV + 1, dtype=jnp.int32)
    return jnp.arange(LEAVES, dtype=jnp.int32)[:, None] + shifts


def draw_far_mid(key, part):
    key = jax.random.fold_in(key, 53)
    reach = LEAF_DEV // 2
    shifts = jax.random.randint(key, (LEAVES // 2, FAR), -reach, reach + 1, dtype=jnp.int32)
    return jnp.arange(LEAVES // 2, dtype=jnp.int32)[:, None] + shifts


def draw_far_top(key, part):
    key = jax.random.fold_in(key, 67)
    first_key, second_key = jax.random.split(key)
    owners = LEAVES // LEAF_DEV
    per_owner = LEAF_DEV // 4
    picked = jax.random.randint(first_key, (owners, owners), 0, per_owner, dtype=jnp.int32)
    candidates = jnp.arange(owners, dtype=jnp.int32)[None, :] * per_owner + picked
    which = jax.random.randint(second_key, (owners, per_owner * FAR), 0, owners, dtype=jnp.int32)
    chosen = jnp.take_along_axis(candidates, which, axis=1)
    return chosen.reshape(LEAVES // 4, FAR).astype(jnp.int32)


def steps_of(rng, extent, cuts, low, top_value):
    def one(axis_at, shards_of):
        heights = jax.random.uniform(jax.random.fold_in(jax.random.fold_in(rng, 6), axis_at), (shards_of,), jnp.float32, low / len(cuts), top_value / len(cuts))
        return jnp.repeat(jnp.exp(heights), extent[axis_at] // shards_of).reshape((-1,) + (1,) * (len(extent) - axis_at - 1))

    factor_of = one(*cuts[0])
    for cut in cuts[1:]:
        factor_of = factor_of * one(*cut)
    return factor_of


def bell_draw(rng, extent, width, most, cuts=(), kind=jnp.bfloat16):
    gain = steps_of(rng, extent, cuts, -0.22, 0.18) if cuts else 1.0
    entries = jax.random.normal(rng, extent, jnp.float32) * width * gain
    return jnp.minimum(jnp.maximum(entries, -most), most).astype(kind)


def setup_inputs(seed: int = 0, part: int = 0) -> dict:
    seeds = jax.random.split(jax.random.key(seed), 15)
    part_splits = jax.random.split(jax.random.fold_in(seeds[14], part), 15)
    coords = jnp.clip(8.0 * jax.random.uniform(part_splits[0], (3, NPTS), jnp.float32) ** steps_of(part_splits[0], (3, NPTS), ((1, 16),), -0.2, 0.2), 0.0, 8.0).astype(jnp.bfloat16)
    probes = bell_draw(part_splits[1], (PROBES, NPTS), 1.0, 6.0, ((1, 16),))
    order = draw_order(jax.random.fold_in(jax.random.fold_in(seeds[14], part), 71), part)
    near_list = draw_near_list(jax.random.fold_in(jax.random.fold_in(seeds[14], part), 71), part)
    near_count = draw_near_count(jax.random.fold_in(jax.random.fold_in(seeds[14], part), 71), part)
    leaf_basis = bell_draw(part_splits[5], (LEAVES, RANK, LEAF), LEAF ** -0.5, 0.375, ((0, 16),))
    transfer_low = bell_draw(part_splits[6], (LEAVES, RANK, RANK), (2 * RANK) ** -0.5, 0.5, ((0, 16),))
    transfer_top = bell_draw(part_splits[7], (LEAVES // 2, RANK, RANK), (2 * RANK) ** -0.5, 0.5, ((0, 16),))
    coupling_leaf = bell_draw(part_splits[8], (LEAVES, FAR, RANK, RANK), (FAR * RANK) ** -0.5, 0.1875, ((0, 16),))
    coupling_mid = bell_draw(part_splits[9], (LEAVES // 2, FAR, RANK, RANK), (FAR * RANK) ** -0.5, 0.1875, ((0, 16),))
    coupling_top = bell_draw(part_splits[10], (LEAVES // 4, FAR, RANK, RANK), (FAR * RANK) ** -0.5, 0.1875, ((0, 16),))
    far_leaf = draw_far_leaf(jax.random.fold_in(jax.random.fold_in(seeds[14], part), 71), part)
    far_mid = draw_far_mid(jax.random.fold_in(jax.random.fold_in(seeds[14], part), 71), part)
    far_top = draw_far_top(jax.random.fold_in(jax.random.fold_in(seeds[14], part), 71), part)
    return {"coords": coords, "probes": probes, "order": order, "near_list": near_list, "near_count": near_count, "leaf_basis": leaf_basis, "transfer_low": transfer_low, "transfer_top": transfer_top, "coupling_leaf": coupling_leaf, "coupling_mid": coupling_mid, "coupling_top": coupling_top, "far_leaf": far_leaf, "far_mid": far_mid, "far_top": far_top}


AMPLITUDE = 0.125
LENGTH_SCALE = 1.0

def kernel_tiles(target, source):
    running = jnp.zeros((source.shape[1], target.shape[1], source.shape[2]), jnp.float32)
    for axis_id in range(3):
        spacing = target[axis_id].astype(jnp.float32)[None, :, None] - source[axis_id].astype(jnp.float32)[:, None, :]
        running = running + spacing * spacing
    return (AMPLITUDE * jnp.exp(-jnp.sqrt(running) / LENGTH_SCALE)).astype(jnp.bfloat16)

def couple(coefficients, partner_lists, coupling, halo_width):
    node_count = partner_lists.shape[0]
    padded = jnp.pad(coefficients, ((halo_width, halo_width), (0, 0), (0, 0)))
    block_size = math.gcd(node_count, 32)

    def per_block(inputs):
        positions, matrices = inputs
        sources = padded[positions + halo_width].astype(jnp.float32)
        return jnp.einsum('nfpr,nfrs->nps', sources, matrices.astype(jnp.float32))
    blocked = lax.map(per_block, (partner_lists.reshape((node_count // block_size, block_size) + partner_lists.shape[1:]), coupling.reshape((node_count // block_size, block_size) + coupling.shape[1:])))
    return blocked.reshape((node_count,) + blocked.shape[2:])

def lift(child, transfer):
    terms = jnp.einsum('lpr,lrs->lps', child.astype(jnp.float32), transfer.astype(jnp.float32))
    return terms.reshape((child.shape[0] // 2, 2) + terms.shape[1:]).sum(axis=1).astype(jnp.bfloat16)

def lower(parent_rounded, transfer, couple_child):
    paired = transfer.reshape((parent_rounded.shape[0], 2) + transfer.shape[1:])
    moved = jnp.einsum('mpr,mcqr->mcpq', parent_rounded.astype(jnp.float32), paired.astype(jnp.float32))
    return (couple_child + moved.reshape(couple_child.shape)).astype(jnp.bfloat16)

def reference(coords, probes, order, near_list, near_count, leaf_basis, transfer_low, transfer_top, coupling_leaf, coupling_mid, coupling_top, far_leaf, far_mid, far_top):
    tree_coords = coords[:, order]
    tree_probes = probes[:, order]
    coord_blocks = tree_coords.reshape(3, LEAVES, LEAF)
    probe_blocks = tree_probes.reshape(PROBES, LEAVES, LEAF)
    padded_coords = jnp.pad(coord_blocks, ((0, 0), (LEAF_DEV, LEAF_DEV), (0, 0)))
    padded_probes = jnp.pad(probe_blocks, ((0, 0), (LEAF_DEV, LEAF_DEV), (0, 0)))

    def near_leaf(inputs):
        neighbors, live_count, target = inputs
        positions = neighbors + LEAF_DEV
        source_coords = jnp.take(padded_coords, positions, axis=1)
        source_probes = jnp.take(padded_probes, positions, axis=1)
        kernel_block = kernel_tiles(target, source_coords)
        live_mask = (jnp.arange(NEAR, dtype=jnp.int32) < live_count).astype(jnp.float32)
        masked_values = source_probes.astype(jnp.float32) * live_mask[None, :, None]
        return jnp.einsum('nts,pns->pt', kernel_block.astype(jnp.float32), masked_values)
    near_blocks = lax.map(near_leaf, (near_list, near_count, jnp.moveaxis(coord_blocks, 1, 0)))
    near_field = jnp.moveaxis(near_blocks, 0, 1).reshape(PROBES, NPTS)
    coeff_leaf = jnp.einsum('plq,lrq->lpr', probe_blocks.astype(jnp.float32), leaf_basis.astype(jnp.float32)).astype(jnp.bfloat16)
    coeff_mid = lift(coeff_leaf, transfer_low)
    coeff_top = lift(coeff_mid, transfer_top)
    couple_leaf = couple(coeff_leaf, far_leaf, coupling_leaf, LEAF_DEV)
    couple_mid = couple(coeff_mid, far_mid, coupling_mid, LEAF_DEV // 2)
    couple_top = couple(coeff_top, far_top, coupling_top, 0)
    top_rounded = couple_top.astype(jnp.bfloat16)
    down_mid = lower(top_rounded, transfer_top, couple_mid)
    down_leaf = lower(down_mid, transfer_low, couple_leaf)
    far_field = jnp.einsum('lpr,lrq->plq', down_leaf.astype(jnp.float32), leaf_basis.astype(jnp.float32)).reshape(PROBES, NPTS)
    return jnp.zeros((PROBES, NPTS), jnp.float32).at[:, order].set(near_field + far_field)
```

```python
import jax
import jax.numpy as jnp
from jax import lax
from jax.experimental import pallas as pl
from jax.experimental.pallas import tpu as pltpu
from jax.sharding import PartitionSpec as P

LEAF = 256
AMPLITUDE = 0.125
LENGTH_SCALE = 1.0
GROUP = 4
FEATURES = 48
BF16 = jnp.bfloat16
F32 = jnp.float32
NT = (((1,), (1,)), ((), ()))


def dot(a, b):
    return jnp.dot(a, b, preferred_element_type=F32)


def dot_nt(a, b):
    return lax.dot_general(a, b, NT, preferred_element_type=F32)


def prep_kernel(
    order, near_count, coords, probes, near_list, basis, low, top,
    points_out, coef_out, counts_out, rows_in, rows_out,
):
    points = coords.shape[1]
    probe_rows = probes.shape[0]
    leaves = basis.shape[0]
    spans = lax.axis_size("col")
    device = lax.axis_index("col")

    for c in range(points // 256):
        at = slice(c * 256, c * 256 + 256)
        block = jnp.concatenate(
            [
                probes[:, at].astype(F32),
                coords[:, at].astype(F32),
                jnp.zeros((125 - probe_rows, 256), F32),
            ],
            axis=0,
        )
        rows_in[at, :] = block.T

    first = device * points

    @pl.loop(0, points // 16)
    def _(k):
        base = pl.multiple_of(k * 16, 16)
        for u in range(16):
            rows_out[pl.ds(base + u, 1), :] = rows_in[pl.ds(order[base + u] - first, 1), :]

    for c in range(points // 256):
        at = slice(c * 256, c * 256 + 256)
        points_out[:, at] = rows_out[at, :].T[:80, :].astype(BF16)

    lane = lax.broadcasted_iota(jnp.int32, (leaves, 128), 1)
    row = lax.broadcasted_iota(jnp.int32, (leaves, 128), 0)
    live = jnp.zeros((leaves, 128), jnp.int32)
    for i in range(leaves):
        live = jnp.where(row == i, near_count[i], live)
    start = device * leaves - leaves
    total = jnp.zeros((leaves, 128), jnp.int32)
    for k in range(near_list.shape[1]):
        named = near_list[:, k : k + 1] - start
        total = total + jnp.where((named == lane) & (live > k), 1, 0)
    inside = (lane + start >= 0) & (lane + start < spans * leaves)
    counts_out[...] = jnp.where(inside, total, 0)

    leaf_coef = [
        dot_nt(points_out[:probe_rows, i * LEAF : (i + 1) * LEAF], basis[i]).astype(BF16)
        for i in range(leaves)
    ]
    mid_coef = [
        (dot(leaf_coef[2 * m], low[2 * m]) + dot(leaf_coef[2 * m + 1], low[2 * m + 1])).astype(BF16)
        for m in range(leaves // 2)
    ]
    top_coef = [
        (dot(mid_coef[2 * q], top[2 * q]) + dot(mid_coef[2 * q + 1], top[2 * q + 1])).astype(BF16)
        for q in range(leaves // 4)
    ]
    nodes = leaf_coef + mid_coef + top_coef
    for m in range(len(nodes) // 2):
        coef_out[m] = jnp.concatenate([nodes[2 * m], nodes[2 * m + 1]], axis=1)


def target_features(cells):
    squares = cells * cells
    high = squares.astype(BF16).astype(F32)
    ones = jnp.ones_like(cells)
    return jnp.concatenate([cells, high, squares - high, ones, ones, jnp.zeros_like(cells)], axis=0)


def source_features(cells):
    squares = cells * cells
    high = squares.astype(BF16).astype(F32)
    ones = jnp.ones_like(cells)
    return jnp.concatenate(
        [-2.0 * cells, ones, ones, high, squares - high, jnp.zeros_like(cells)], axis=0
    )


def fill_targets(points, targets):
    for i in range(targets.shape[0]):
        cells = points[64:80, i * LEAF : (i + 1) * LEAF].astype(F32)[:8]
        targets[i] = target_features(cells).astype(BF16)


def fill_sources(points, sources, values, place):
    leaves = points.shape[1] // LEAF
    for i in range(leaves):
        cells = points[64:80, i * LEAF : (i + 1) * LEAF].astype(F32)[:8]
        sources[place + i] = source_features(cells).T.astype(BF16)
        values[place + i] = points[:64, i * LEAF : (i + 1) * LEAF]


def list_pairs(counts, listed, windows):
    leaves = counts.shape[0]
    position = jnp.int32(0)
    for i in range(leaves):
        for lane, slot in windows(i):
            count = counts[i, lane]
            listed[position] = count * 4096 + (i * 64 + slot)
            position = position + jnp.minimum(count, 1)
    for u in range(GROUP):
        listed[position + u] = jnp.int32(0)
    return (position + (GROUP - 1)) // GROUP


def add_pairs(listed, groups, targets, sources, values, field):
    @pl.loop(0, groups)
    def _(g):
        for u in range(GROUP):
            pair = listed[g * GROUP + u]
            slot = pair & 63
            leaf = (pair >> 6) & 63
            weight = (pair >> 12).astype(F32) * AMPLITUDE
            squared = jnp.maximum(dot(sources[slot], targets[leaf]), 1e-30)
            tile = jnp.exp(squared * lax.rsqrt(squared) * (-1.0 / LENGTH_SCALE)).astype(BF16)
            field[leaf] += dot(values[slot], tile) * weight


def own_kernel(counts, points, field, targets, sources, values, listed):
    leaves = targets.shape[0]
    fill_targets(points, targets)
    fill_sources(points, sources, values, 0)
    field[...] = jnp.zeros_like(field)
    groups = list_pairs(counts, listed, lambda i: [(leaves + j, j) for j in range(leaves)])
    add_pairs(listed, groups, targets, sources, values, field)


def rest_kernel(
    counts, order, far_leaf, far_mid, far_top,
    own, left, right, field_in, coef_own, coef_left, coef_right, tops,
    basis, low, top, couple_leaf_hbm, couple_mid_hbm, couple_top_hbm,
    out,
    targets, sources, values, listed, field,
    around_leaf, around_mid, around_top, couple_leaf, couple_mid, couple_top,
    couple_sum, rows_in, rows_out, sems,
):
    leaves = basis.shape[0]
    points = own.shape[1]
    device = lax.axis_index("col")
    copies = [
        pltpu.make_async_copy(couple_top_hbm, couple_top, sems.at[0]),
        pltpu.make_async_copy(couple_mid_hbm, couple_mid, sems.at[1]),
        pltpu.make_async_copy(couple_leaf_hbm, couple_leaf, sems.at[2]),
    ]
    for copy in copies:
        copy.start()

    fill_targets(own, targets)
    fill_sources(left, sources, values, 0)
    fill_sources(right, sources, values, leaves)
    field[...] = field_in[...]
    groups = list_pairs(
        counts,
        listed,
        lambda i: [(j, j) for j in range(i, leaves)]
        + [(2 * leaves + j, leaves + j) for j in range(i + 1)],
    )
    add_pairs(listed, groups, targets, sources, values, field)

    def spread(pair, around, slot):
        one, two = pair[:, :64], pair[:, 64:]
        around[slot] = jnp.concatenate([one, one], axis=1)
        around[slot + 1] = jnp.concatenate([two, two], axis=1)

    mids = leaves // 2
    for part, coefs in enumerate((coef_left, coef_own, coef_right)):
        for m in range(leaves // 2):
            spread(coefs[m], around_leaf, part * leaves + 2 * m)
        for m in range(mids // 2):
            spread(coefs[leaves // 2 + m], around_mid, part * mids + 2 * m)

    @pl.loop(0, tops.shape[0])
    def _(m):
        spread(tops[m], around_top, 2 * m)

    for copy in copies:
        copy.wait()

    lower_half = lax.broadcasted_iota(jnp.int32, (64, 128), 1) < 64

    def couple(lists, around, matrices, base, place):
        far = lists.shape[1]

        @pl.loop(0, lists.shape[0])
        def _(n):
            total = jnp.zeros((64, 64), F32)
            for f in range(0, far, 4):
                picked = [around[lists[n, f + d] - base] for d in range(4)]
                rows = jnp.concatenate(
                    [
                        jnp.where(lower_half, picked[0], picked[1]),
                        jnp.where(lower_half, picked[2], picked[3]),
                    ],
                    axis=1,
                )
                total = total + dot(rows, matrices[n, f : f + 4].reshape(256, 64))
            couple_sum[place + n] = total

    couple(far_top, around_top, couple_top, 0, leaves + mids)
    couple(far_mid, around_mid, couple_mid, device * mids - mids, leaves)
    couple(far_leaf, around_leaf, couple_leaf, device * leaves - leaves, 0)

    for m in range(mids):
        parent = couple_sum[leaves + mids + m // 2].astype(BF16)
        couple_sum[leaves + m] += dot_nt(parent, top[m])
    for i in range(leaves):
        parent = couple_sum[leaves + i // 2].astype(BF16)
        couple_sum[i] += dot_nt(parent, low[i])
    for i in range(leaves):
        total = field[i] + dot(couple_sum[i].astype(BF16), basis[i])
        rows_in[i * LEAF : (i + 1) * LEAF, :] = jnp.concatenate(
            [total, jnp.zeros_like(total)], axis=0
        ).T

    first = device * points

    @pl.loop(0, points // 16)
    def _(k):
        base = pl.multiple_of(k * 16, 16)
        for u in range(16):
            rows_out[pl.ds(order[base + u] - first, 1), :] = rows_in[pl.ds(base + u, 1), :]

    for c in range(points // 256):
        at = slice(c * 256, c * 256 + 256)
        out[:, at] = rows_out[at, :].T[:64, :]


def vmem():
    return pl.BlockSpec(memory_space=pltpu.VMEM)


def smem():
    return pl.BlockSpec(memory_space=pltpu.SMEM)


def params():
    return pltpu.CompilerParams(vmem_limit_bytes=50 * 2**20)


def per_device(
    coords, probes, order, near_list, near_count, leaf_basis, transfer_low, transfer_top,
    coupling_leaf, coupling_mid, coupling_top, far_leaf, far_mid, far_top,
):
    points = coords.shape[1]
    leaves = leaf_basis.shape[0]
    mids, tops = leaves // 2, leaves // 4
    count = lax.axis_size("col")
    shape = jax.ShapeDtypeStruct

    tree, coef, counts = pl.pallas_call(
        prep_kernel,
        out_shape=(
            shape((80, points), BF16),
            shape(((leaves + mids + tops) // 2, 64, 128), BF16),
            shape((leaves, 128), jnp.int32),
        ),
        in_specs=[smem(), smem()] + [vmem()] * 6,
        out_specs=(vmem(), vmem(), vmem()),
        scratch_shapes=[pltpu.VMEM((points, 128), F32)] * 2,
        compiler_params=params(),
        cost_estimate=pl.CostEstimate(flops=10**9, bytes_accessed=2 * 10**7, transcendentals=0),
        name="prep",
    )(order, near_count, coords, probes, near_list, leaf_basis, transfer_low, transfer_top)

    ahead = [(i, i + 1) for i in range(count - 1)]
    back = [(i + 1, i) for i in range(count - 1)]
    shared = coef[: (leaves + mids) // 2]
    left = lax.ppermute(tree, "col", ahead)
    right = lax.ppermute(tree, "col", back)
    coef_left = lax.ppermute(shared, "col", ahead)
    coef_right = lax.ppermute(shared, "col", back)
    gathered = lax.all_gather(coef[(leaves + mids) // 2 :], "col", axis=0, tiled=True)

    field = pl.pallas_call(
        own_kernel,
        out_shape=shape((leaves, 64, LEAF), F32),
        in_specs=[smem(), vmem()],
        out_specs=vmem(),
        scratch_shapes=[
            pltpu.VMEM((leaves, FEATURES, LEAF), BF16),
            pltpu.VMEM((leaves, LEAF, FEATURES), BF16),
            pltpu.VMEM((leaves, 64, LEAF), BF16),
            pltpu.SMEM((leaves * leaves + GROUP,), jnp.int32),
        ],
        compiler_params=params(),
        cost_estimate=pl.CostEstimate(
            flops=2 * 10**10, bytes_accessed=2 * 10**7, transcendentals=10**7
        ),
        name="own_pairs",
    )(counts, tree)

    return pl.pallas_call(
        rest_kernel,
        out_shape=shape((64, points), F32),
        in_specs=[smem()] * 5 + [vmem()] * 11 + [pl.BlockSpec(memory_space=pl.ANY)] * 3,
        out_specs=vmem(),
        scratch_shapes=[
            pltpu.VMEM((leaves, FEATURES, LEAF), BF16),
            pltpu.VMEM((2 * leaves, LEAF, FEATURES), BF16),
            pltpu.VMEM((2 * leaves, 64, LEAF), BF16),
            pltpu.SMEM((leaves * (leaves + 1) + GROUP,), jnp.int32),
            pltpu.VMEM((leaves, 64, LEAF), F32),
            pltpu.VMEM((3 * leaves, 64, 128), BF16),
            pltpu.VMEM((3 * mids, 64, 128), BF16),
            pltpu.VMEM((tops * count, 64, 128), BF16),
            pltpu.VMEM(coupling_leaf.shape, BF16),
            pltpu.VMEM(coupling_mid.shape, BF16),
            pltpu.VMEM(coupling_top.shape, BF16),
            pltpu.VMEM((leaves + mids + tops, 64, 64), F32),
            pltpu.VMEM((points, 128), F32),
            pltpu.VMEM((points, 128), F32),
            pltpu.SemaphoreType.DMA((3,)),
        ],
        compiler_params=params(),
        cost_estimate=pl.CostEstimate(
            flops=2 * 10**10, bytes_accessed=2 * 10**7, transcendentals=10**7
        ),
        name="rest",
    )(
        counts, order, far_leaf, far_mid, far_top,
        tree, left, right, field, coef, coef_left, coef_right, gathered,
        leaf_basis, transfer_low, transfer_top, coupling_leaf, coupling_mid, coupling_top,
    )


def solution(mesh):
    both = ("groups", "col")
    return jax.shard_map(
        per_device,
        mesh=mesh,
        in_specs=(
            P(None, both),
            P(None, both),
            P(both),
            P(both, None),
            P(both),
            P(both, None, None),
            P(both, None, None),
            P(both, None, None),
            P(both, None, None, None),
            P(both, None, None, None),
            P(both, None, None, None),
            P(both, None),
            P(both, None),
            P(both, None),
        ),
        out_specs=P(None, both),
        check_vma=False,
    )
```

```python
import jax
import jax.numpy as jnp
from jax import lax
from jax.experimental import pallas as pl
from jax.experimental.pallas import tpu as pltpu
from jax.sharding import PartitionSpec as P

LEAF = 256
AMPLITUDE = 0.125
LENGTH_SCALE = 1.0
GROUP = 16
FEATURES = 48
BF16 = jnp.bfloat16
F32 = jnp.float32
MESH = pl.DeviceIdType.MESH
VMEM_BYTES = 60 * 2**20
NT = (((1,), (1,)), ((), ()))


def dot(a, b):
    return jnp.dot(a, b, preferred_element_type=F32)


def dot_nt(a, b):
    return lax.dot_general(a, b, NT, preferred_element_type=F32)


def within(position, points):
    if points & (points - 1) == 0:
        return position & (points - 1)
    return lax.rem(position, points)


def prep_kernel(
    order, near_count, coords, probes, near_list, basis_hbm, low_hbm, top_hbm,
    points_out, coef_out, counts_out, left, right, coef_left, coef_right, tops,
    rows_in, rows_out, basis, low, top,
    load_sems, send_sems, recv_sems, top_send, top_recv, pair_send, pair_recv,
):
    points = coords.shape[1]
    probe_rows = probes.shape[0]
    leaves = basis.shape[0]
    spans = lax.axis_size("col")
    device = lax.axis_index("col")
    chips = spans // 2
    chip, side = device // 2, device % 2
    shared = coef_left.shape[0]

    barrier = pltpu.get_barrier_semaphore()

    def greet(to):
        pl.semaphore_signal(barrier, inc=1, device_id={"col": to}, device_id_type=MESH)

    @pl.loop(1, chips)
    def _(j):
        greet(((chip + j) % chips) * 2 + side)

    greet(chip * 2 + 1 - side)
    outer = jnp.where(side == 0, device - 1, device + 1)
    has_outer = (outer >= 0) & (outer < spans)

    @pl.when(has_outer)
    def _():
        greet(outer)

    loads = [
        pltpu.make_async_copy(basis_hbm, basis, load_sems.at[0]),
        pltpu.make_async_copy(low_hbm, low, load_sems.at[1]),
        pltpu.make_async_copy(top_hbm, top, load_sems.at[2]),
    ]
    for load in loads:
        load.start()

    for c in range(points // 256):
        at = slice(c * 256, c * 256 + 256)
        block = jnp.concatenate(
            [
                probes[:, at].astype(F32),
                coords[:, at].astype(F32),
                jnp.zeros((125 - probe_rows, 256), F32),
            ],
            axis=0,
        )
        rows_in[at, :] = block.T

    @pl.loop(0, points // 16)
    def _(k):
        base = pl.multiple_of(k * 16, 16)
        for u in range(16):
            rows_out[pl.ds(base + u, 1), :] = rows_in[pl.ds(within(order[base + u], points), 1), :]

    for c in range(points // 256):
        at = slice(c * 256, c * 256 + 256)
        points_out[:, at] = rows_out[at, :].T[:80, :].astype(BF16)

    pl.semaphore_wait(barrier, chips + jnp.where(has_outer, 1, 0))

    def put(source, target, k, to):
        return pltpu.make_async_remote_copy(
            src_ref=source,
            dst_ref=target,
            send_sem=send_sems.at[k],
            recv_sem=recv_sems.at[k],
            device_id={"col": to},
            device_id_type=MESH,
        )

    ahead, behind = jnp.minimum(device + 1, spans - 1), jnp.maximum(device - 1, 0)
    points_ahead = put(points_out, left, 0, ahead)
    points_behind = put(points_out, right, 1, behind)
    coef_ahead = put(coef_out.at[pl.ds(0, shared)], coef_left, 2, ahead)
    coef_behind = put(coef_out.at[pl.ds(0, shared)], coef_right, 3, behind)
    is_first, is_last = device == 0, device == spans - 1

    @pl.when(jnp.logical_not(is_last))
    def _():
        points_ahead.start()

    @pl.when(jnp.logical_not(is_first))
    def _():
        points_behind.start()

    for load in loads:
        load.wait()

    leaf_coef = [
        dot_nt(points_out[:probe_rows, i * LEAF : (i + 1) * LEAF], basis[i]).astype(BF16)
        for i in range(leaves)
    ]
    mid_coef = [
        (dot(leaf_coef[2 * m], low[2 * m]) + dot(leaf_coef[2 * m + 1], low[2 * m + 1])).astype(BF16)
        for m in range(leaves // 2)
    ]
    top_coef = [
        (dot(mid_coef[2 * q], top[2 * q]) + dot(mid_coef[2 * q + 1], top[2 * q + 1])).astype(BF16)
        for q in range(leaves // 4)
    ]
    nodes = leaf_coef + mid_coef
    for m in range(len(nodes) // 2):
        coef_out[m] = jnp.concatenate([nodes[2 * m], nodes[2 * m + 1]], axis=1)
    for q in range(leaves // 8):
        tops[side, chip, q] = jnp.concatenate([top_coef[2 * q], top_coef[2 * q + 1]], axis=1)

    def spread_top(j):
        return pltpu.make_async_remote_copy(
            src_ref=tops.at[side, chip],
            dst_ref=tops.at[side, chip],
            send_sem=top_send.at[j],
            recv_sem=top_recv.at[j],
            device_id={"col": ((chip + j) % chips) * 2 + side},
            device_id_type=MESH,
        )

    @pl.loop(1, chips)
    def _(j):
        spread_top(j).start()

    @pl.when(jnp.logical_not(is_last))
    def _():
        coef_ahead.start()

    @pl.when(jnp.logical_not(is_first))
    def _():
        coef_behind.start()

    lane = lax.broadcasted_iota(jnp.int32, (leaves, 128), 1)
    row = lax.broadcasted_iota(jnp.int32, (leaves, 128), 0)
    live = jnp.zeros((leaves, 128), jnp.int32)
    for i in range(leaves):
        live = jnp.where(row == i, near_count[i], live)
    start = device * leaves - leaves
    total = jnp.zeros((leaves, 128), jnp.int32)
    for k in range(near_list.shape[1]):
        named = near_list[:, k : k + 1] - start
        total = total + jnp.where((named == lane) & (live > k), 1, 0)
    inside = (lane + start >= 0) & (lane + start < spans * leaves)
    counts_out[...] = jnp.where(inside, total, 0)

    @pl.loop(1, chips)
    def _(j):
        spread_top(j).wait()

    pair = pltpu.make_async_remote_copy(
        src_ref=tops.at[side],
        dst_ref=tops.at[side],
        send_sem=pair_send,
        recv_sem=pair_recv,
        device_id={"col": chip * 2 + 1 - side},
        device_id_type=MESH,
    )
    pair.start()

    @pl.when(jnp.logical_not(is_last))
    def _():
        points_ahead.wait_send()
        coef_ahead.wait_send()
        points_behind.wait_recv()
        coef_behind.wait_recv()

    @pl.when(jnp.logical_not(is_first))
    def _():
        points_behind.wait_send()
        coef_behind.wait_send()
        points_ahead.wait_recv()
        coef_ahead.wait_recv()

    pair.wait()


def target_features(cells):
    squares = cells * cells
    high = squares.astype(BF16).astype(F32)
    ones = jnp.ones_like(cells)
    return jnp.concatenate([cells, high, squares - high, ones, ones, jnp.zeros_like(cells)], axis=0)


def source_features(cells):
    squares = cells * cells
    high = squares.astype(BF16).astype(F32)
    ones = jnp.ones_like(cells)
    return jnp.concatenate(
        [-2.0 * cells, ones, ones, high, squares - high, jnp.zeros_like(cells)], axis=0
    )


def fill_targets(points, targets):
    for i in range(targets.shape[0]):
        cells = points[64:80, i * LEAF : (i + 1) * LEAF].astype(F32)[:8]
        targets[i] = target_features(cells).astype(BF16)


def fill_sources(points, sources, values, place):
    leaves = points.shape[1] // LEAF
    for i in range(leaves):
        cells = points[64:80, i * LEAF : (i + 1) * LEAF].astype(F32)[:8]
        sources[place + i] = source_features(cells).T.astype(BF16)
        values[place + i] = points[:64, i * LEAF : (i + 1) * LEAF]


def list_pairs(counts, listed, leaves):
    def one(i, position):
        for j in range(2 * leaves + 1):
            count = counts[i, i + j]
            listed[position] = count * 4096 + (i * 64 + i + j)
            position = position + jnp.minimum(count, 1)
        return position

    position = lax.fori_loop(0, leaves, one, jnp.int32(0))
    for u in range(GROUP):
        listed[position + u] = jnp.int32(leaves)
    return (position + (GROUP - 1)) // GROUP


def add_pairs(listed, groups, targets, sources, values, field):
    @pl.loop(0, groups)
    def _(g):
        pairs = [listed[g * GROUP + u] for u in range(GROUP)]
        slots = [pair & 63 for pair in pairs]
        owners = [(pair >> 6) & 63 for pair in pairs]
        weights = [(pair >> 12).astype(F32) * AMPLITUDE for pair in pairs]
        tiles = []
        for u in range(GROUP):
            squared = jnp.maximum(dot(sources[slots[u]], targets[owners[u]]), 1e-30)
            distance = squared * lax.rsqrt(squared)
            tiles.append(jnp.exp(distance * (-1.0 / LENGTH_SCALE)).astype(BF16))
        sums = [dot(values[slots[u]], tiles[u]) * weights[u] for u in range(GROUP)]
        for u in range(GROUP):
            field[owners[u]] += sums[u]


def apply_kernel(
    counts, order, far_leaf, far_mid, far_top,
    own, left, right, coef_own, coef_left, coef_right, tops,
    basis, low, top, couple_leaf_hbm, couple_mid_hbm, couple_top_hbm,
    out,
    targets, sources, values, listed, field,
    around_leaf, around_mid, around_top, couple_leaf, couple_mid, couple_top,
    couple_sum, rows_in, rows_out, sems,
):
    leaves = basis.shape[0]
    points = own.shape[1]
    device = lax.axis_index("col")
    spans = lax.axis_size("col")
    copies = [
        pltpu.make_async_copy(couple_top_hbm, couple_top, sems.at[0]),
        pltpu.make_async_copy(couple_mid_hbm, couple_mid, sems.at[1]),
        pltpu.make_async_copy(couple_leaf_hbm, couple_leaf, sems.at[2]),
    ]
    for copy in copies:
        copy.start()

    fill_targets(own, targets)
    fill_sources(left, sources, values, 0)
    fill_sources(own, sources, values, leaves)
    fill_sources(right, sources, values, 2 * leaves)
    field[...] = jnp.zeros_like(field)
    groups = list_pairs(counts, listed, leaves)
    add_pairs(listed, groups, targets, sources, values, field)

    def spread(pair, around, slot):
        one, two = pair[:, :64], pair[:, 64:]
        around[slot] = jnp.concatenate([one, one], axis=1)
        around[slot + 1] = jnp.concatenate([two, two], axis=1)

    mids, quads = leaves // 2, leaves // 4

    def spread_part(coefs, part):
        for m in range(leaves // 2):
            spread(coefs[m], around_leaf, part * leaves + 2 * m)
        for m in range(mids // 2):
            spread(coefs[leaves // 2 + m], around_mid, part * mids + 2 * m)

    spread_part(coef_own, 1)
    for coefs, part, missing in (
        (coef_left, 0, device == 0),
        (coef_right, 2, device == spans - 1),
    ):

        @pl.when(missing)
        def _(part=part):
            at_leaf, at_mid = pl.ds(part * leaves, leaves), pl.ds(part * mids, mids)
            around_leaf[at_leaf] = jnp.zeros((leaves, 64, 128), BF16)
            around_mid[at_mid] = jnp.zeros((mids, 64, 128), BF16)

        @pl.when(jnp.logical_not(missing))
        def _(coefs=coefs, part=part):
            spread_part(coefs, part)

    @pl.loop(0, tops.shape[1])
    def _(chip):
        for side in range(2):
            for q in range(quads // 2):
                spread(tops[side, chip, q], around_top, (2 * chip + side) * quads + 2 * q)

    for copy in copies:
        copy.wait()

    lower_half = lax.broadcasted_iota(jnp.int32, (64, 128), 1) < 64

    def couple(lists, around, matrices, base, place):
        far = lists.shape[1]

        @pl.loop(0, lists.shape[0] // 4)
        def _(block):
            totals = []
            for d in range(4):
                n = block * 4 + d
                total = None
                for f in range(0, far, 4):
                    picked = [around[lists[n, f + e] - base] for e in range(4)]
                    rows = jnp.concatenate(
                        [
                            jnp.where(lower_half, picked[0], picked[1]),
                            jnp.where(lower_half, picked[2], picked[3]),
                        ],
                        axis=1,
                    )
                    term = dot(rows, matrices[n, f : f + 4].reshape(256, 64))
                    total = term if total is None else total + term
                totals.append(total)
            for d in range(4):
                couple_sum[place + block * 4 + d] = totals[d]

    couple(far_top, around_top, couple_top, 0, leaves + mids)
    couple(far_mid, around_mid, couple_mid, device * mids - mids, leaves)
    couple(far_leaf, around_leaf, couple_leaf, device * leaves - leaves, 0)

    upper = [couple_sum[leaves + mids + q].astype(BF16) for q in range(quads)]
    middle = [
        (couple_sum[leaves + m] + dot_nt(upper[m // 2], top[m])).astype(BF16) for m in range(mids)
    ]
    bottom = [
        (couple_sum[i] + dot_nt(middle[i // 2], low[i])).astype(BF16) for i in range(leaves)
    ]
    for i in range(leaves):
        total = field[i] + dot(bottom[i], basis[i])
        rows_in[i * LEAF : (i + 1) * LEAF, :] = jnp.concatenate(
            [total, jnp.zeros_like(total)], axis=0
        ).T

    @pl.loop(0, points // 16)
    def _(k):
        base = pl.multiple_of(k * 16, 16)
        for u in range(16):
            rows_out[pl.ds(within(order[base + u], points), 1), :] = rows_in[pl.ds(base + u, 1), :]

    for c in range(points // 256):
        at = slice(c * 256, c * 256 + 256)
        out[:, at] = rows_out[at, :].T[:64, :]


def vmem():
    return pl.BlockSpec(memory_space=pltpu.VMEM)


def smem():
    return pl.BlockSpec(memory_space=pltpu.SMEM)


def hbm():
    return pl.BlockSpec(memory_space=pl.ANY)


def per_device(
    coords, probes, order, near_list, near_count, leaf_basis, transfer_low, transfer_top,
    coupling_leaf, coupling_mid, coupling_top, far_leaf, far_mid, far_top,
):
    points = coords.shape[1]
    leaves = leaf_basis.shape[0]
    mids, tops = leaves // 2, leaves // 4
    count = lax.axis_size("col")
    chips = count // 2
    shape = jax.ShapeDtypeStruct
    shared = (leaves + mids) // 2
    dma = pltpu.SemaphoreType.DMA

    exchanged = pl.pallas_call(
        prep_kernel,
        out_shape=(
            shape((80, points), BF16),
            shape((shared, 64, 128), BF16),
            shape((leaves, 128), jnp.int32),
            shape((80, points), BF16),
            shape((80, points), BF16),
            shape((shared, 64, 128), BF16),
            shape((shared, 64, 128), BF16),
            shape((2, chips, tops // 2, 64, 128), BF16),
        ),
        in_specs=[smem(), smem()] + [vmem()] * 3 + [hbm()] * 3,
        out_specs=(vmem(),) * 8,
        scratch_shapes=[
            pltpu.VMEM((points, 128), F32),
            pltpu.VMEM((points, 128), F32),
            pltpu.VMEM(leaf_basis.shape, BF16),
            pltpu.VMEM(transfer_low.shape, BF16),
            pltpu.VMEM(transfer_top.shape, BF16),
            dma((3,)),
            dma((4,)),
            dma((4,)),
            dma((chips,)),
            dma((chips,)),
            dma,
            dma,
        ],
        compiler_params=pltpu.CompilerParams(
            vmem_limit_bytes=VMEM_BYTES, collective_id=0, has_side_effects=True
        ),
        cost_estimate=pl.CostEstimate(flops=10**9, bytes_accessed=2 * 10**7, transcendentals=0),
        name="prep",
    )(order, near_count, coords, probes, near_list, leaf_basis, transfer_low, transfer_top)
    tree, coef, counts, left, right, coef_left, coef_right, gathered = exchanged

    return pl.pallas_call(
        apply_kernel,
        out_shape=shape((64, points), F32),
        in_specs=[smem()] * 5 + [vmem()] * 10 + [hbm()] * 3,
        out_specs=vmem(),
        scratch_shapes=[
            pltpu.VMEM((leaves, FEATURES, LEAF), BF16),
            pltpu.VMEM((3 * leaves, LEAF, FEATURES), BF16),
            pltpu.VMEM((3 * leaves, 64, LEAF), BF16),
            pltpu.SMEM((leaves * (2 * leaves + 1) + GROUP,), jnp.int32),
            pltpu.VMEM((leaves, 64, LEAF), F32),
            pltpu.VMEM((3 * leaves, 64, 128), BF16),
            pltpu.VMEM((3 * mids, 64, 128), BF16),
            pltpu.VMEM((tops * count, 64, 128), BF16),
            pltpu.VMEM(coupling_leaf.shape, BF16),
            pltpu.VMEM(coupling_mid.shape, BF16),
            pltpu.VMEM(coupling_top.shape, BF16),
            pltpu.VMEM((leaves + mids + tops, 64, 64), F32),
            pltpu.VMEM((points, 128), F32),
            pltpu.VMEM((points, 128), F32),
            pltpu.SemaphoreType.DMA((3,)),
        ],
        compiler_params=pltpu.CompilerParams(vmem_limit_bytes=VMEM_BYTES),
        cost_estimate=pl.CostEstimate(
            flops=2 * 10**10, bytes_accessed=2 * 10**7, transcendentals=10**7
        ),
        name="apply",
    )(
        counts, order, far_leaf, far_mid, far_top,
        tree, left, right, coef, coef_left, coef_right, gathered,
        leaf_basis, transfer_low, transfer_top, coupling_leaf, coupling_mid, coupling_top,
    )


def solution(mesh):
    both = ("groups", "col")
    return jax.shard_map(
        per_device,
        mesh=mesh,
        in_specs=(
            P(None, both),
            P(None, both),
            P(both),
            P(both, None),
            P(both),
            P(both, None, None),
            P(both, None, None),
            P(both, None, None),
            P(both, None, None, None),
            P(both, None, None, None),
            P(both, None, None, None),
            P(both, None),
            P(both, None),
            P(both, None),
        ),
        out_specs=P(None, both),
        check_vma=False,
    )
```

```python
import jax
import jax.numpy as jnp
from jax import lax
from jax.experimental import pallas as pl
from jax.experimental.pallas import tpu as pltpu
from jax.sharding import PartitionSpec as P

LEAF = 256
AMPLITUDE = 0.125
LENGTH_SCALE = 1.0
GROUP = 16
CHUNKS = 4
FEATURES = 48
BF16 = jnp.bfloat16
F32 = jnp.float32
MESH = pl.DeviceIdType.MESH
VMEM_BYTES = 60 * 2**20
NT = (((1,), (1,)), ((), ()))


def dot(a, b):
    return jnp.dot(a, b, preferred_element_type=F32)


def dot_nt(a, b):
    return lax.dot_general(a, b, NT, preferred_element_type=F32)


def within(position, points):
    if points & (points - 1) == 0:
        return position & (points - 1)
    return lax.rem(position, points)


def prep_kernel(
    order, near_count, coords, probes, near_list, basis_hbm, low_hbm, top_hbm,
    points_out, cells_out, coef_out, counts_out,
    left, right, cells_left, cells_right, coef_left, coef_right, tops,
    rows_in, rows_out, basis, low, top,
    load_sems, send_sems, recv_sems, top_send, top_recv, pair_send, pair_recv,
):
    points = coords.shape[1]
    probe_rows = probes.shape[0]
    leaves = basis.shape[0]
    spans = lax.axis_size("col")
    device = lax.axis_index("col")
    chips = spans // 2
    chip, side = device // 2, device % 2

    barrier = pltpu.get_barrier_semaphore()

    def greet(to):
        pl.semaphore_signal(barrier, inc=1, device_id={"col": to}, device_id_type=MESH)

    @pl.loop(1, chips)
    def _(j):
        greet(((chip + j) % chips) * 2 + side)

    greet(chip * 2 + 1 - side)
    outer = jnp.where(side == 0, device - 1, device + 1)
    has_outer = (outer >= 0) & (outer < spans)

    @pl.when(has_outer)
    def _():
        greet(outer)

    loads = [
        pltpu.make_async_copy(basis_hbm, basis, load_sems.at[0]),
        pltpu.make_async_copy(low_hbm, low, load_sems.at[1]),
        pltpu.make_async_copy(top_hbm, top, load_sems.at[2]),
    ]
    for load in loads:
        load.start()

    for c in range(points // 256):
        at = slice(c * 256, c * 256 + 256)
        block = jnp.concatenate(
            [
                probes[:, at].astype(F32),
                coords[:, at].astype(F32),
                jnp.zeros((125 - probe_rows, 256), F32),
            ],
            axis=0,
        )
        rows_in[at, :] = block.T

    def put(source, target, k, to):
        return pltpu.make_async_remote_copy(
            src_ref=source,
            dst_ref=target,
            send_sem=send_sems.at[k],
            recv_sem=recv_sems.at[k],
            device_id={"col": to},
            device_id_type=MESH,
        )

    ahead, behind = jnp.minimum(device + 1, spans - 1), jnp.maximum(device - 1, 0)
    is_first, is_last = device == 0, device == spans - 1
    width = points // CHUNKS
    parts = [slice(c * width, c * width + width) for c in range(CHUNKS)]
    to_ahead = [put(points_out.at[:, p], left.at[:, p], c, ahead) for c, p in enumerate(parts)]
    to_ahead.append(put(cells_out, cells_left, CHUNKS, ahead))
    to_ahead.append(put(coef_out, coef_left, CHUNKS + 1, ahead))
    base_sem = CHUNKS + 2
    to_behind = [
        put(points_out.at[:, p], right.at[:, p], base_sem + c, behind) for c, p in enumerate(parts)
    ]
    to_behind.append(put(cells_out, cells_right, base_sem + CHUNKS, behind))
    to_behind.append(put(coef_out, coef_right, base_sem + CHUNKS + 1, behind))

    def launch(c):
        @pl.when(jnp.logical_not(is_last))
        def _():
            to_ahead[c].start()

        @pl.when(jnp.logical_not(is_first))
        def _():
            to_behind[c].start()

    cells = []
    for c in range(CHUNKS):

        @pl.loop(0, width // 16)
        def _(k, c=c):
            base = pl.multiple_of(c * width + k * 16, 16)
            for u in range(16):
                rows_out[pl.ds(base + u, 1), :] = rows_in[
                    pl.ds(within(order[base + u], points), 1), :
                ]

        for d in range(width // LEAF):
            at = slice(c * width + d * LEAF, c * width + d * LEAF + LEAF)
            turned = rows_out[at, :].T
            points_out[:, at] = turned[:probe_rows].astype(BF16)
            cells.append(turned[probe_rows : probe_rows + 4])
        if c == 0:
            pl.semaphore_wait(barrier, chips + jnp.where(has_outer, 1, 0))
        launch(c)

    columns = leaves // 4
    for j in range(columns):
        cells_out[:, j * LEAF : (j + 1) * LEAF] = jnp.concatenate(
            [cells[g * columns + j] for g in range(4)], axis=0
        ).astype(BF16)
    launch(CHUNKS)

    for load in loads:
        load.wait()

    leaf_coef = [
        dot_nt(points_out[:probe_rows, i * LEAF : (i + 1) * LEAF], basis[i]).astype(BF16)
        for i in range(leaves)
    ]
    mid_coef = [
        (dot(leaf_coef[2 * m], low[2 * m]) + dot(leaf_coef[2 * m + 1], low[2 * m + 1])).astype(BF16)
        for m in range(leaves // 2)
    ]
    top_coef = [
        (dot(mid_coef[2 * q], top[2 * q]) + dot(mid_coef[2 * q + 1], top[2 * q + 1])).astype(BF16)
        for q in range(leaves // 4)
    ]
    nodes = leaf_coef + mid_coef
    for m in range(len(nodes) // 2):
        coef_out[m] = jnp.concatenate([nodes[2 * m], nodes[2 * m + 1]], axis=1)
    for q in range(leaves // 8):
        tops[side, chip, q] = jnp.concatenate([top_coef[2 * q], top_coef[2 * q + 1]], axis=1)

    def spread_top(j):
        return pltpu.make_async_remote_copy(
            src_ref=tops.at[side, chip],
            dst_ref=tops.at[side, chip],
            send_sem=top_send.at[j],
            recv_sem=top_recv.at[j],
            device_id={"col": ((chip + j) % chips) * 2 + side},
            device_id_type=MESH,
        )

    @pl.loop(1, chips)
    def _(j):
        spread_top(j).start()

    launch(CHUNKS + 1)

    lane = lax.broadcasted_iota(jnp.int32, (leaves, 128), 1)
    row = lax.broadcasted_iota(jnp.int32, (leaves, 128), 0)
    live = jnp.zeros((leaves, 128), jnp.int32)
    for i in range(leaves):
        live = jnp.where(row == i, near_count[i], live)
    start = device * leaves - leaves
    total = jnp.zeros((leaves, 128), jnp.int32)
    for k in range(near_list.shape[1]):
        named = near_list[:, k : k + 1] - start
        total = total + jnp.where((named == lane) & (live > k), 1, 0)
    inside = (lane + start >= 0) & (lane + start < spans * leaves)
    counts_out[...] = jnp.where(inside, total, 0)

    @pl.loop(1, chips)
    def _(j):
        spread_top(j).wait()

    pair = pltpu.make_async_remote_copy(
        src_ref=tops.at[side],
        dst_ref=tops.at[side],
        send_sem=pair_send,
        recv_sem=pair_recv,
        device_id={"col": chip * 2 + 1 - side},
        device_id_type=MESH,
    )
    pair.start()

    @pl.when(jnp.logical_not(is_last))
    def _():
        for c in range(CHUNKS + 2):
            to_ahead[c].wait_send()
            to_behind[c].wait_recv()

    @pl.when(jnp.logical_not(is_first))
    def _():
        for c in range(CHUNKS + 2):
            to_behind[c].wait_send()
            to_ahead[c].wait_recv()

    pair.wait()


def target_features(cells):
    squares = cells * cells
    high = squares.astype(BF16).astype(F32)
    ones = jnp.ones_like(cells)
    return jnp.concatenate([cells, high, squares - high, ones, ones, jnp.zeros_like(cells)], axis=0)


def source_features(cells):
    squares = cells * cells
    high = squares.astype(BF16).astype(F32)
    ones = jnp.ones_like(cells)
    return jnp.concatenate(
        [-2.0 * cells, ones, ones, high, squares - high, jnp.zeros_like(cells)], axis=0
    )


def leaf_cells(packed, i):
    columns = packed.shape[1] // LEAF
    g, j = i // columns, i % columns
    cells = packed[:, j * LEAF : (j + 1) * LEAF].astype(F32)[4 * g : 4 * g + 4]
    return jnp.concatenate([cells, jnp.zeros_like(cells)], axis=0)


def fill_targets(packed, targets):
    for i in range(targets.shape[0]):
        targets[i] = target_features(leaf_cells(packed, i)).astype(BF16)


def fill_sources(points, packed, sources, values, place):
    for i in range(points.shape[1] // LEAF):
        sources[place + i] = source_features(leaf_cells(packed, i)).T.astype(BF16)
        values[place + i] = points[:, i * LEAF : (i + 1) * LEAF]


def list_pairs(counts, listed, leaves):
    def one(i, position):
        for j in range(2 * leaves + 1):
            count = counts[i, i + j]
            listed[position] = count * 4096 + (i * 64 + i + j)
            position = position + jnp.minimum(count, 1)
        return position

    position = lax.fori_loop(0, leaves, one, jnp.int32(0))
    for u in range(GROUP):
        listed[position + u] = jnp.int32(leaves)
    return (position + (GROUP - 1)) // GROUP


def add_pairs(listed, groups, targets, sources, values, field):
    @pl.loop(0, groups)
    def _(g):
        pairs = [listed[g * GROUP + u] for u in range(GROUP)]
        slots = [pair & 63 for pair in pairs]
        owners = [(pair >> 6) & 63 for pair in pairs]
        weights = [(pair >> 12).astype(F32) * AMPLITUDE for pair in pairs]
        tiles = []
        for u in range(GROUP):
            squared = jnp.maximum(dot(sources[slots[u]], targets[owners[u]]), 1e-30)
            distance = squared * lax.rsqrt(squared)
            tiles.append(jnp.exp(distance * (-1.0 / LENGTH_SCALE)).astype(BF16))
        sums = [dot(values[slots[u]], tiles[u]) * weights[u] for u in range(GROUP)]
        for u in range(GROUP):
            field[owners[u]] += sums[u]


def apply_kernel(
    counts, order, far_leaf, far_mid, far_top,
    own, left, right, cells_own, cells_left, cells_right,
    coef_own, coef_left, coef_right, tops,
    basis, low, top, couple_leaf_hbm, couple_mid_hbm, couple_top_hbm,
    out,
    targets, sources, values, listed, field,
    around_leaf, around_mid, around_top, couple_leaf, couple_mid, couple_top,
    couple_sum, rows_in, rows_out, sems,
):
    leaves = basis.shape[0]
    points = own.shape[1]
    device = lax.axis_index("col")
    spans = lax.axis_size("col")
    copies = [
        pltpu.make_async_copy(couple_top_hbm, couple_top, sems.at[0]),
        pltpu.make_async_copy(couple_mid_hbm, couple_mid, sems.at[1]),
        pltpu.make_async_copy(couple_leaf_hbm, couple_leaf, sems.at[2]),
    ]
    for copy in copies:
        copy.start()

    fill_targets(cells_own, targets)
    fill_sources(left, cells_left, sources, values, 0)
    fill_sources(own, cells_own, sources, values, leaves)
    fill_sources(right, cells_right, sources, values, 2 * leaves)
    field[...] = jnp.zeros_like(field)
    groups = list_pairs(counts, listed, leaves)
    add_pairs(listed, groups, targets, sources, values, field)

    def spread(pair, around, slot):
        one, two = pair[:, :64], pair[:, 64:]
        around[slot] = jnp.concatenate([one, one], axis=1)
        around[slot + 1] = jnp.concatenate([two, two], axis=1)

    mids, quads = leaves // 2, leaves // 4

    def spread_part(coefs, part):
        for m in range(leaves // 2):
            spread(coefs[m], around_leaf, part * leaves + 2 * m)
        for m in range(mids // 2):
            spread(coefs[leaves // 2 + m], around_mid, part * mids + 2 * m)

    spread_part(coef_own, 1)
    for coefs, part, missing in (
        (coef_left, 0, device == 0),
        (coef_right, 2, device == spans - 1),
    ):

        @pl.when(missing)
        def _(part=part):
            at_leaf, at_mid = pl.ds(part * leaves, leaves), pl.ds(part * mids, mids)
            around_leaf[at_leaf] = jnp.zeros((leaves, 64, 128), BF16)
            around_mid[at_mid] = jnp.zeros((mids, 64, 128), BF16)

        @pl.when(jnp.logical_not(missing))
        def _(coefs=coefs, part=part):
            spread_part(coefs, part)

    @pl.loop(0, tops.shape[1])
    def _(chip):
        for side in range(2):
            for q in range(quads // 2):
                spread(tops[side, chip, q], around_top, (2 * chip + side) * quads + 2 * q)

    for copy in copies:
        copy.wait()

    lower_half = lax.broadcasted_iota(jnp.int32, (64, 128), 1) < 64

    def couple(lists, around, matrices, base, place):
        far = lists.shape[1]

        @pl.loop(0, lists.shape[0] // 4)
        def _(block):
            totals = []
            for d in range(4):
                n = block * 4 + d
                total = None
                for f in range(0, far, 4):
                    picked = [around[lists[n, f + e] - base] for e in range(4)]
                    rows = jnp.concatenate(
                        [
                            jnp.where(lower_half, picked[0], picked[1]),
                            jnp.where(lower_half, picked[2], picked[3]),
                        ],
                        axis=1,
                    )
                    term = dot(rows, matrices[n, f : f + 4].reshape(256, 64))
                    total = term if total is None else total + term
                totals.append(total)
            for d in range(4):
                couple_sum[place + block * 4 + d] = totals[d]

    couple(far_top, around_top, couple_top, 0, leaves + mids)
    couple(far_mid, around_mid, couple_mid, device * mids - mids, leaves)
    couple(far_leaf, around_leaf, couple_leaf, device * leaves - leaves, 0)

    upper = [couple_sum[leaves + mids + q].astype(BF16) for q in range(quads)]
    middle = [
        (couple_sum[leaves + m] + dot_nt(upper[m // 2], top[m])).astype(BF16) for m in range(mids)
    ]
    bottom = [
        (couple_sum[i] + dot_nt(middle[i // 2], low[i])).astype(BF16) for i in range(leaves)
    ]
    for i in range(leaves):
        total = field[i] + dot(bottom[i], basis[i])
        rows_in[i * LEAF : (i + 1) * LEAF, :] = jnp.concatenate(
            [total, jnp.zeros_like(total)], axis=0
        ).T

    @pl.loop(0, points // 16)
    def _(k):
        base = pl.multiple_of(k * 16, 16)
        for u in range(16):
            rows_out[pl.ds(within(order[base + u], points), 1), :] = rows_in[pl.ds(base + u, 1), :]

    for c in range(points // 256):
        at = slice(c * 256, c * 256 + 256)
        out[:, at] = rows_out[at, :].T[:64, :]


def vmem():
    return pl.BlockSpec(memory_space=pltpu.VMEM)


def smem():
    return pl.BlockSpec(memory_space=pltpu.SMEM)


def hbm():
    return pl.BlockSpec(memory_space=pl.ANY)


def per_device(
    coords, probes, order, near_list, near_count, leaf_basis, transfer_low, transfer_top,
    coupling_leaf, coupling_mid, coupling_top, far_leaf, far_mid, far_top,
):
    points = coords.shape[1]
    leaves = leaf_basis.shape[0]
    mids, tops = leaves // 2, leaves // 4
    count = lax.axis_size("col")
    chips = count // 2
    shape = jax.ShapeDtypeStruct
    shared = (leaves + mids) // 2
    dma = pltpu.SemaphoreType.DMA

    exchanged = pl.pallas_call(
        prep_kernel,
        out_shape=(
            shape((64, points), BF16),
            shape((16, points // 4), BF16),
            shape((shared, 64, 128), BF16),
            shape((leaves, 128), jnp.int32),
            shape((64, points), BF16),
            shape((64, points), BF16),
            shape((16, points // 4), BF16),
            shape((16, points // 4), BF16),
            shape((shared, 64, 128), BF16),
            shape((shared, 64, 128), BF16),
            shape((2, chips, tops // 2, 64, 128), BF16),
        ),
        in_specs=[smem(), smem()] + [vmem()] * 3 + [hbm()] * 3,
        out_specs=(vmem(),) * 11,
        scratch_shapes=[
            pltpu.VMEM((points, 128), F32),
            pltpu.VMEM((points, 128), F32),
            pltpu.VMEM(leaf_basis.shape, BF16),
            pltpu.VMEM(transfer_low.shape, BF16),
            pltpu.VMEM(transfer_top.shape, BF16),
            dma((3,)),
            dma((2 * CHUNKS + 4,)),
            dma((2 * CHUNKS + 4,)),
            dma((chips,)),
            dma((chips,)),
            dma,
            dma,
        ],
        compiler_params=pltpu.CompilerParams(
            vmem_limit_bytes=VMEM_BYTES, collective_id=0, has_side_effects=True
        ),
        cost_estimate=pl.CostEstimate(flops=10**9, bytes_accessed=2 * 10**7, transcendentals=0),
        name="prep",
    )(order, near_count, coords, probes, near_list, leaf_basis, transfer_low, transfer_top)
    tree, cells, coef, counts, left, right = exchanged[:6]
    cells_left, cells_right, coef_left, coef_right, gathered = exchanged[6:]

    return pl.pallas_call(
        apply_kernel,
        out_shape=shape((64, points), F32),
        in_specs=[smem()] * 5 + [vmem()] * 13 + [hbm()] * 3,
        out_specs=vmem(),
        scratch_shapes=[
            pltpu.VMEM((leaves, FEATURES, LEAF), BF16),
            pltpu.VMEM((3 * leaves, LEAF, FEATURES), BF16),
            pltpu.VMEM((3 * leaves, 64, LEAF), BF16),
            pltpu.SMEM((leaves * (2 * leaves + 1) + GROUP,), jnp.int32),
            pltpu.VMEM((leaves, 64, LEAF), F32),
            pltpu.VMEM((3 * leaves, 64, 128), BF16),
            pltpu.VMEM((3 * mids, 64, 128), BF16),
            pltpu.VMEM((tops * count, 64, 128), BF16),
            pltpu.VMEM(coupling_leaf.shape, BF16),
            pltpu.VMEM(coupling_mid.shape, BF16),
            pltpu.VMEM(coupling_top.shape, BF16),
            pltpu.VMEM((leaves + mids + tops, 64, 64), F32),
            pltpu.VMEM((points, 128), F32),
            pltpu.VMEM((points, 128), F32),
            pltpu.SemaphoreType.DMA((3,)),
        ],
        compiler_params=pltpu.CompilerParams(vmem_limit_bytes=VMEM_BYTES),
        cost_estimate=pl.CostEstimate(
            flops=2 * 10**10, bytes_accessed=2 * 10**7, transcendentals=10**7
        ),
        name="apply",
    )(
        counts, order, far_leaf, far_mid, far_top,
        tree, left, right, cells, cells_left, cells_right, coef, coef_left, coef_right, gathered,
        leaf_basis, transfer_low, transfer_top, coupling_leaf, coupling_mid, coupling_top,
    )


def solution(mesh):
    both = ("groups", "col")
    return jax.shard_map(
        per_device,
        mesh=mesh,
        in_specs=(
            P(None, both),
            P(None, both),
            P(both),
            P(both, None),
            P(both),
            P(both, None, None),
            P(both, None, None),
            P(both, None, None),
            P(both, None, None, None),
            P(both, None, None, None),
            P(both, None, None, None),
            P(both, None),
            P(both, None),
            P(both, None),
        ),
        out_specs=P(None, both),
        check_vma=False,
    )
```

```python
import jax
import jax.numpy as jnp
from jax import lax
from jax.experimental import pallas as pl
from jax.experimental.pallas import tpu as pltpu
from jax.sharding import PartitionSpec as P

LEAF = 256
AMPLITUDE = 0.125
LENGTH_SCALE = 1.0
GROUP = 16
CHUNKS = 4
STEADY = 6
FEATURES = 48
BF16 = jnp.bfloat16
F32 = jnp.float32
MESH = pl.DeviceIdType.MESH
VMEM_BYTES = 60 * 2**20
NT = (((1,), (1,)), ((), ()))


def dot(a, b):
    return jnp.dot(a, b, preferred_element_type=F32)


def dot_nt(a, b):
    return lax.dot_general(a, b, NT, preferred_element_type=F32)


def near_tile(source, target):
    squared = jnp.maximum(dot(source, target), 1e-30)
    distance = squared * lax.rsqrt(squared)
    return jnp.exp(distance * (-1.0 / LENGTH_SCALE)).astype(BF16)


def within(position, points):
    if points & (points - 1) == 0:
        return position & (points - 1)
    return lax.rem(position, points)


def prep_kernel(
    order, near_count, coords, probes, near_list, basis_hbm, low_hbm, top_hbm,
    points_out, cells_out, coef_out, counts_out,
    left, right, cells_left, cells_right, coef_left, coef_right, tops, field_out,
    rows_in, rows_out, basis, low, top, targets, sources, values,
    load_sems, send_sems, recv_sems, top_send, top_recv, pair_send, pair_recv,
):
    points = coords.shape[1]
    probe_rows = probes.shape[0]
    leaves = basis.shape[0]
    spans = lax.axis_size("col")
    device = lax.axis_index("col")
    chips = spans // 2
    chip, side = device // 2, device % 2

    barrier = pltpu.get_barrier_semaphore()

    def greet(to):
        pl.semaphore_signal(barrier, inc=1, device_id={"col": to}, device_id_type=MESH)

    @pl.loop(1, chips)
    def _(j):
        greet(((chip + j) % chips) * 2 + side)

    greet(chip * 2 + 1 - side)
    outer = jnp.where(side == 0, device - 1, device + 1)
    has_outer = (outer >= 0) & (outer < spans)

    @pl.when(has_outer)
    def _():
        greet(outer)

    loads = [
        pltpu.make_async_copy(basis_hbm, basis, load_sems.at[0]),
        pltpu.make_async_copy(low_hbm, low, load_sems.at[1]),
        pltpu.make_async_copy(top_hbm, top, load_sems.at[2]),
    ]
    for load in loads:
        load.start()

    for c in range(points // 256):
        at = slice(c * 256, c * 256 + 256)
        block = jnp.concatenate(
            [
                probes[:, at].astype(F32),
                coords[:, at].astype(F32),
                jnp.zeros((125 - probe_rows, 256), F32),
            ],
            axis=0,
        )
        rows_in[at, :] = block.T

    def put(source, target, k, to):
        return pltpu.make_async_remote_copy(
            src_ref=source,
            dst_ref=target,
            send_sem=send_sems.at[k],
            recv_sem=recv_sems.at[k],
            device_id={"col": to},
            device_id_type=MESH,
        )

    ahead, behind = jnp.minimum(device + 1, spans - 1), jnp.maximum(device - 1, 0)
    is_first, is_last = device == 0, device == spans - 1
    width = points // CHUNKS
    parts = [slice(c * width, c * width + width) for c in range(CHUNKS)]
    to_ahead = [put(points_out.at[:, p], left.at[:, p], c, ahead) for c, p in enumerate(parts)]
    to_ahead.append(put(cells_out, cells_left, CHUNKS, ahead))
    to_ahead.append(put(coef_out, coef_left, CHUNKS + 1, ahead))
    base_sem = CHUNKS + 2
    to_behind = [
        put(points_out.at[:, p], right.at[:, p], base_sem + c, behind) for c, p in enumerate(parts)
    ]
    to_behind.append(put(cells_out, cells_right, base_sem + CHUNKS, behind))
    to_behind.append(put(coef_out, coef_right, base_sem + CHUNKS + 1, behind))

    def launch(c):
        @pl.when(jnp.logical_not(is_last))
        def _():
            to_ahead[c].start()

        @pl.when(jnp.logical_not(is_first))
        def _():
            to_behind[c].start()

    cells = []
    for c in range(CHUNKS):

        @pl.loop(0, width // 16)
        def _(k, c=c):
            base = pl.multiple_of(c * width + k * 16, 16)
            for u in range(16):
                rows_out[pl.ds(base + u, 1), :] = rows_in[
                    pl.ds(within(order[base + u], points), 1), :
                ]

        for d in range(width // LEAF):
            at = slice(c * width + d * LEAF, c * width + d * LEAF + LEAF)
            turned = rows_out[at, :].T
            points_out[:, at] = turned[:probe_rows].astype(BF16)
            cells.append(turned[probe_rows : probe_rows + 4])
        if c == 0:
            pl.semaphore_wait(barrier, chips + jnp.where(has_outer, 1, 0))
        launch(c)

    columns = leaves // 4
    for j in range(columns):
        cells_out[:, j * LEAF : (j + 1) * LEAF] = jnp.concatenate(
            [cells[g * columns + j] for g in range(4)], axis=0
        ).astype(BF16)
    launch(CHUNKS)

    for load in loads:
        load.wait()

    leaf_coef = [
        dot_nt(points_out[:probe_rows, i * LEAF : (i + 1) * LEAF], basis[i]).astype(BF16)
        for i in range(leaves)
    ]
    mid_coef = [
        (dot(leaf_coef[2 * m], low[2 * m]) + dot(leaf_coef[2 * m + 1], low[2 * m + 1])).astype(BF16)
        for m in range(leaves // 2)
    ]
    top_coef = [
        (dot(mid_coef[2 * q], top[2 * q]) + dot(mid_coef[2 * q + 1], top[2 * q + 1])).astype(BF16)
        for q in range(leaves // 4)
    ]
    nodes = leaf_coef + mid_coef
    for m in range(len(nodes) // 2):
        coef_out[m] = jnp.concatenate([nodes[2 * m], nodes[2 * m + 1]], axis=1)
    for q in range(leaves // 8):
        tops[side, chip, q] = jnp.concatenate([top_coef[2 * q], top_coef[2 * q + 1]], axis=1)

    def spread_top(j):
        return pltpu.make_async_remote_copy(
            src_ref=tops.at[side, chip],
            dst_ref=tops.at[side, chip],
            send_sem=top_send.at[j],
            recv_sem=top_recv.at[j],
            device_id={"col": ((chip + j) % chips) * 2 + side},
            device_id_type=MESH,
        )

    @pl.loop(1, chips)
    def _(j):
        spread_top(j).start()

    launch(CHUNKS + 1)

    lane = lax.broadcasted_iota(jnp.int32, (leaves, 128), 1)
    row = lax.broadcasted_iota(jnp.int32, (leaves, 128), 0)
    live = jnp.zeros((leaves, 128), jnp.int32)
    for i in range(leaves):
        live = jnp.where(row == i, near_count[i], live)
    start = device * leaves - leaves
    total = jnp.zeros((leaves, 128), jnp.int32)
    for k in range(near_list.shape[1]):
        named = near_list[:, k : k + 1] - start
        total = total + jnp.where((named == lane) & (live > k), 1, 0)
    inside = (lane + start >= 0) & (lane + start < spans * leaves)
    total = jnp.where(inside, total, 0)
    counts_out[...] = total

    fill_targets(cells_out, targets)
    fill_sources(points_out, cells_out, sources, values, 0)
    field_out[...] = jnp.zeros_like(field_out)

    def steady(lo, hi):
        @pl.loop(lo, hi)
        def _(d):
            chosen = lane == leaves + (row + d) % leaves
            weight = jnp.sum(jnp.where(chosen, total, 0).astype(F32), axis=1, keepdims=True)
            weight = weight * AMPLITUDE
            slots = [(i + d) % leaves for i in range(leaves)]
            tiles = [near_tile(sources[slots[i]], targets[i]) for i in range(leaves)]
            sums = [dot(values[slots[i]], tiles[i]) * weight[i : i + 1] for i in range(leaves)]
            for i in range(leaves):
                field_out[i] += sums[i]

    steady(0, STEADY // 2)

    @pl.loop(1, chips)
    def _(j):
        spread_top(j).wait()

    pair = pltpu.make_async_remote_copy(
        src_ref=tops.at[side],
        dst_ref=tops.at[side],
        send_sem=pair_send,
        recv_sem=pair_recv,
        device_id={"col": chip * 2 + 1 - side},
        device_id_type=MESH,
    )
    pair.start()
    steady(STEADY // 2, STEADY)

    @pl.when(jnp.logical_not(is_last))
    def _():
        for c in range(CHUNKS + 2):
            to_ahead[c].wait_send()
            to_behind[c].wait_recv()

    @pl.when(jnp.logical_not(is_first))
    def _():
        for c in range(CHUNKS + 2):
            to_behind[c].wait_send()
            to_ahead[c].wait_recv()

    pair.wait()


def target_features(cells):
    squares = cells * cells
    high = squares.astype(BF16).astype(F32)
    ones = jnp.ones_like(cells)
    return jnp.concatenate([cells, high, squares - high, ones, ones, jnp.zeros_like(cells)], axis=0)


def source_features(cells):
    squares = cells * cells
    high = squares.astype(BF16).astype(F32)
    ones = jnp.ones_like(cells)
    return jnp.concatenate(
        [-2.0 * cells, ones, ones, high, squares - high, jnp.zeros_like(cells)], axis=0
    )


def leaf_cells(packed, i):
    columns = packed.shape[1] // LEAF
    g, j = i // columns, i % columns
    cells = packed[:, j * LEAF : (j + 1) * LEAF].astype(F32)[4 * g : 4 * g + 4]
    return jnp.concatenate([cells, jnp.zeros_like(cells)], axis=0)


def fill_targets(packed, targets):
    for i in range(targets.shape[0]):
        targets[i] = target_features(leaf_cells(packed, i)).astype(BF16)


def fill_sources(points, packed, sources, values, place):
    for i in range(points.shape[1] // LEAF):
        sources[place + i] = source_features(leaf_cells(packed, i)).T.astype(BF16)
        values[place + i] = points[:, i * LEAF : (i + 1) * LEAF]


def list_pairs(counts, listed, leaves):
    def one(i, position):
        for j in range(2 * leaves + 1):
            count = counts[i, i + j]
            if (j - leaves) % leaves < STEADY:
                count = jnp.where((i + j >= leaves) & (i + j < 2 * leaves), 0, count)
            listed[position] = count * 4096 + (i * 64 + i + j)
            position = position + jnp.minimum(count, 1)
        return position

    position = lax.fori_loop(0, leaves, one, jnp.int32(0))
    for u in range(GROUP):
        listed[position + u] = jnp.int32(leaves)
    return (position + (GROUP - 1)) // GROUP


def add_pairs(listed, groups, targets, sources, values, field):
    @pl.loop(0, groups)
    def _(g):
        pairs = [listed[g * GROUP + u] for u in range(GROUP)]
        slots = [pair & 63 for pair in pairs]
        owners = [(pair >> 6) & 63 for pair in pairs]
        weights = [(pair >> 12).astype(F32) * AMPLITUDE for pair in pairs]
        tiles = [near_tile(sources[slots[u]], targets[owners[u]]) for u in range(GROUP)]
        sums = [dot(values[slots[u]], tiles[u]) * weights[u] for u in range(GROUP)]
        for u in range(GROUP):
            field[owners[u]] += sums[u]


def apply_kernel(
    counts, order, far_leaf, far_mid, far_top,
    own, left, right, cells_own, cells_left, cells_right,
    coef_own, coef_left, coef_right, tops, field_in,
    basis, low, top, couple_leaf_hbm, couple_mid_hbm, couple_top_hbm,
    out,
    targets, sources, values, listed, field,
    around_leaf, around_mid, around_top, couple_leaf, couple_mid, couple_top,
    couple_sum, rows_in, rows_out, sems,
):
    leaves = basis.shape[0]
    points = own.shape[1]
    device = lax.axis_index("col")
    spans = lax.axis_size("col")
    copies = [
        pltpu.make_async_copy(couple_top_hbm, couple_top, sems.at[0]),
        pltpu.make_async_copy(couple_mid_hbm, couple_mid, sems.at[1]),
        pltpu.make_async_copy(couple_leaf_hbm, couple_leaf, sems.at[2]),
    ]
    for copy in copies:
        copy.start()

    fill_targets(cells_own, targets)
    fill_sources(left, cells_left, sources, values, 0)
    fill_sources(own, cells_own, sources, values, leaves)
    fill_sources(right, cells_right, sources, values, 2 * leaves)
    field[...] = field_in[...]
    groups = list_pairs(counts, listed, leaves)
    add_pairs(listed, groups, targets, sources, values, field)

    def spread(pair, around, slot):
        one, two = pair[:, :64], pair[:, 64:]
        around[slot] = jnp.concatenate([one, one], axis=1)
        around[slot + 1] = jnp.concatenate([two, two], axis=1)

    mids, quads = leaves // 2, leaves // 4

    def spread_part(coefs, part):
        for m in range(leaves // 2):
            spread(coefs[m], around_leaf, part * leaves + 2 * m)
        for m in range(mids // 2):
            spread(coefs[leaves // 2 + m], around_mid, part * mids + 2 * m)

    spread_part(coef_own, 1)
    for coefs, part, missing in (
        (coef_left, 0, device == 0),
        (coef_right, 2, device == spans - 1),
    ):

        @pl.when(missing)
        def _(part=part):
            at_leaf, at_mid = pl.ds(part * leaves, leaves), pl.ds(part * mids, mids)
            around_leaf[at_leaf] = jnp.zeros((leaves, 64, 128), BF16)
            around_mid[at_mid] = jnp.zeros((mids, 64, 128), BF16)

        @pl.when(jnp.logical_not(missing))
        def _(coefs=coefs, part=part):
            spread_part(coefs, part)

    @pl.loop(0, tops.shape[1])
    def _(chip):
        for side in range(2):
            for q in range(quads // 2):
                spread(tops[side, chip, q], around_top, (2 * chip + side) * quads + 2 * q)

    for copy in copies:
        copy.wait()

    lower_half = lax.broadcasted_iota(jnp.int32, (64, 128), 1) < 64

    def couple(lists, around, matrices, base, place):
        far = lists.shape[1]

        @pl.loop(0, lists.shape[0] // 4)
        def _(block):
            totals = []
            for d in range(4):
                n = block * 4 + d
                total = None
                for f in range(0, far, 4):
                    picked = [around[lists[n, f + e] - base] for e in range(4)]
                    rows = jnp.concatenate(
                        [
                            jnp.where(lower_half, picked[0], picked[1]),
                            jnp.where(lower_half, picked[2], picked[3]),
                        ],
                        axis=1,
                    )
                    term = dot(rows, matrices[n, f : f + 4].reshape(256, 64))
                    total = term if total is None else total + term
                totals.append(total)
            for d in range(4):
                couple_sum[place + block * 4 + d] = totals[d]

    couple(far_top, around_top, couple_top, 0, leaves + mids)
    couple(far_mid, around_mid, couple_mid, device * mids - mids, leaves)
    couple(far_leaf, around_leaf, couple_leaf, device * leaves - leaves, 0)

    upper = [couple_sum[leaves + mids + q].astype(BF16) for q in range(quads)]
    middle = [
        (couple_sum[leaves + m] + dot_nt(upper[m // 2], top[m])).astype(BF16) for m in range(mids)
    ]
    bottom = [
        (couple_sum[i] + dot_nt(middle[i // 2], low[i])).astype(BF16) for i in range(leaves)
    ]
    for i in range(leaves):
        total = field[i] + dot(bottom[i], basis[i])
        rows_in[i * LEAF : (i + 1) * LEAF, :] = jnp.concatenate(
            [total, jnp.zeros_like(total)], axis=0
        ).T

    @pl.loop(0, points // 16)
    def _(k):
        base = pl.multiple_of(k * 16, 16)
        for u in range(16):
            rows_out[pl.ds(within(order[base + u], points), 1), :] = rows_in[pl.ds(base + u, 1), :]

    for c in range(points // 256):
        at = slice(c * 256, c * 256 + 256)
        out[:, at] = rows_out[at, :].T[:64, :]


def vmem():
    return pl.BlockSpec(memory_space=pltpu.VMEM)


def smem():
    return pl.BlockSpec(memory_space=pltpu.SMEM)


def hbm():
    return pl.BlockSpec(memory_space=pl.ANY)


def per_device(
    coords, probes, order, near_list, near_count, leaf_basis, transfer_low, transfer_top,
    coupling_leaf, coupling_mid, coupling_top, far_leaf, far_mid, far_top,
):
    points = coords.shape[1]
    leaves = leaf_basis.shape[0]
    mids, tops = leaves // 2, leaves // 4
    count = lax.axis_size("col")
    chips = count // 2
    shape = jax.ShapeDtypeStruct
    shared = (leaves + mids) // 2
    dma = pltpu.SemaphoreType.DMA

    exchanged = pl.pallas_call(
        prep_kernel,
        out_shape=(
            shape((64, points), BF16),
            shape((16, points // 4), BF16),
            shape((shared, 64, 128), BF16),
            shape((leaves, 128), jnp.int32),
            shape((64, points), BF16),
            shape((64, points), BF16),
            shape((16, points // 4), BF16),
            shape((16, points // 4), BF16),
            shape((shared, 64, 128), BF16),
            shape((shared, 64, 128), BF16),
            shape((2, chips, tops // 2, 64, 128), BF16),
            shape((leaves, 64, LEAF), F32),
        ),
        in_specs=[smem(), smem()] + [vmem()] * 3 + [hbm()] * 3,
        out_specs=(vmem(),) * 12,
        scratch_shapes=[
            pltpu.VMEM((points, 128), F32),
            pltpu.VMEM((points, 128), F32),
            pltpu.VMEM(leaf_basis.shape, BF16),
            pltpu.VMEM(transfer_low.shape, BF16),
            pltpu.VMEM(transfer_top.shape, BF16),
            pltpu.VMEM((leaves, FEATURES, LEAF), BF16),
            pltpu.VMEM((leaves, LEAF, FEATURES), BF16),
            pltpu.VMEM((leaves, 64, LEAF), BF16),
            dma((3,)),
            dma((2 * CHUNKS + 4,)),
            dma((2 * CHUNKS + 4,)),
            dma((chips,)),
            dma((chips,)),
            dma,
            dma,
        ],
        compiler_params=pltpu.CompilerParams(
            vmem_limit_bytes=VMEM_BYTES, collective_id=0, has_side_effects=True
        ),
        cost_estimate=pl.CostEstimate(flops=10**9, bytes_accessed=2 * 10**7, transcendentals=0),
        name="prep",
    )(order, near_count, coords, probes, near_list, leaf_basis, transfer_low, transfer_top)
    tree, cells, coef, counts, left, right = exchanged[:6]
    cells_left, cells_right, coef_left, coef_right, gathered, field = exchanged[6:]

    return pl.pallas_call(
        apply_kernel,
        out_shape=shape((64, points), F32),
        in_specs=[smem()] * 5 + [vmem()] * 14 + [hbm()] * 3,
        out_specs=vmem(),
        scratch_shapes=[
            pltpu.VMEM((leaves, FEATURES, LEAF), BF16),
            pltpu.VMEM((3 * leaves, LEAF, FEATURES), BF16),
            pltpu.VMEM((3 * leaves, 64, LEAF), BF16),
            pltpu.SMEM((leaves * (2 * leaves + 1) + GROUP,), jnp.int32),
            pltpu.VMEM((leaves, 64, LEAF), F32),
            pltpu.VMEM((3 * leaves, 64, 128), BF16),
            pltpu.VMEM((3 * mids, 64, 128), BF16),
            pltpu.VMEM((tops * count, 64, 128), BF16),
            pltpu.VMEM(coupling_leaf.shape, BF16),
            pltpu.VMEM(coupling_mid.shape, BF16),
            pltpu.VMEM(coupling_top.shape, BF16),
            pltpu.VMEM((leaves + mids + tops, 64, 64), F32),
            pltpu.VMEM((points, 128), F32),
            pltpu.VMEM((points, 128), F32),
            pltpu.SemaphoreType.DMA((3,)),
        ],
        compiler_params=pltpu.CompilerParams(vmem_limit_bytes=VMEM_BYTES),
        cost_estimate=pl.CostEstimate(
            flops=2 * 10**10, bytes_accessed=2 * 10**7, transcendentals=10**7
        ),
        name="apply",
    )(
        counts, order, far_leaf, far_mid, far_top,
        tree, left, right, cells, cells_left, cells_right, coef, coef_left, coef_right, gathered, field,
        leaf_basis, transfer_low, transfer_top, coupling_leaf, coupling_mid, coupling_top,
    )


def solution(mesh):
    both = ("groups", "col")
    return jax.shard_map(
        per_device,
        mesh=mesh,
        in_specs=(
            P(None, both),
            P(None, both),
            P(both),
            P(both, None),
            P(both),
            P(both, None, None),
            P(both, None, None),
            P(both, None, None),
            P(both, None, None, None),
            P(both, None, None, None),
            P(both, None, None, None),
            P(both, None),
            P(both, None),
            P(both, None),
        ),
        out_specs=P(None, both),
        check_vma=False,
    )
```
